32 devices in a mesh: gx: 2 (over x), gy: 4 (over z), ga: 4 (over y, core).
Axes of the slice: x: 2, y: 2, z: 4, core: 2. Of those that a mesh axis runs over, the one named last changes fastest.
Arguments:
- fixed: float32 [16, 32, 512], P('gx', 'gy', 'ga'), may hold values from -6 to 6
- moving: float32 [16, 32, 512], P('gx', 'gy', 'ga'), may hold values from -6 to 6
- coarse_disp: float32 [3, 4, 8, 128], P(None, 'gx', 'gy', 'ga'), may hold values from -6 to 6
- offsets: int32 [3, 4, 8, 128], P(None, 'gx', 'gy', 'ga'), may hold values from -2 to 1
Outputs:
- similarity: float32 [], replicated
- grad_coarse: float32 [3, 4, 8, 128], P(None, 'gx', 'gy', 'ga')
The draws below stay inside these ranges and needn't reach their ends.
All inputs are finite; a program needn't handle non-finite values.
Results may differ from the reference program's by a relative error of at most 0.0003.
Values sent between devices are 32-bit elements; how exact they have to be, the bound alone decides.
A program may use at most 64 MiB of HBM per device.

```python
import jax
import jax.numpy as jnp
from jax import lax

NX = 16
NY = 32
NZ = 512
KX = 4
KY = 8
KZ = 128


def image_pair(key):
    shape = (NX, NY, NZ)
    first_key = jax.random.fold_in(key, 11)
    second_key = jax.random.fold_in(key, 12)
    source = jnp.clip(jax.random.normal(first_key, shape, jnp.float32), -5.0, 5.0)
    noise = jnp.clip(jax.random.normal(second_key, shape, jnp.float32), -5.0, 5.0)
    ramp = 0.3 + 0.6 * jnp.arange(NX, dtype=jnp.float32)[:, None, None] / max(NX - 1, 1)
    fixed_image = ramp * jnp.roll(source, 1, axis=2) + jnp.sqrt(1.0 - ramp * ramp) * noise
    return (jnp.clip(fixed_image, -6.0, 6.0), jnp.clip(source, -6.0, 6.0))


def draw_fixed(key, part):
    return image_pair(key)[0]


def draw_moving(key, part):
    return image_pair(key)[1]


def with_ends(array, key, smallest, high):
    longest = array.shape.index(max(array.shape))
    spots = []
    for shift in (0, 1):
        where = [jax.random.randint(jax.random.fold_in(key, axis), (), 0, length) for axis, length in enumerate(array.shape)]
        where[longest] = (where[longest] + shift) % array.shape[longest]
        spots.append(tuple(where))
    return array.at[spots[0]].set(smallest).at[spots[1]].set(high)


def levels(own_key, extent, pieces, low, top_value):
    def one(position, shards_of):
        steps = jax.random.uniform(jax.random.fold_in(jax.random.fold_in(own_key, 6), position), (shards_of,), jnp.float32, low / len(pieces), top_value / len(pieces))
        return jnp.repeat(jnp.exp(steps), extent[position] // shards_of).reshape((-1,) + (1,) * (len(extent) - position - 1))

    factor_of = one(*pieces[0])
    for cut in pieces[1:]:
        factor_of = factor_of * one(*cut)
    return factor_of


def bell_draw(stream_key, extent, deviation, bound, pieces=(), kind=jnp.bfloat16):
    loudness = levels(stream_key, extent, pieces, -0.22, 0.18) if pieces else 1.0
    drawn = jax.random.normal(stream_key, extent, jnp.float32) * deviation * loudness
    return jnp.minimum(jnp.maximum(drawn, -bound), bound).astype(kind)


def setup_inputs(seed: int = 0) -> dict:
    key_of = jax.random.split(jax.random.key(seed), 5)
    return {
        "fixed": draw_fixed(jax.random.fold_in(key_of[4], 71), 0),
        "moving": draw_moving(jax.random.fold_in(key_of[4], 71), 0),
        "coarse_disp": bell_draw(key_of[2], (3, KX, KY, KZ), 1.5, 6.0, ((1, 2), (2, 4), (3, 4)), jnp.float32),
        "offsets": with_ends(jax.random.randint(key_of[3], (3, KX, KY, KZ), -2, 2), jax.random.fold_in(key_of[3], 1), -2, 1).astype(jnp.int32),
    }


window_count = 729.0
epsilon = 1e-05

def smooth_padded(padded):
    padded = (padded[:, :-2] + 2.0 * padded[:, 1:-1] + padded[:, 2:]) * 0.25
    padded = (padded[:, :, :-2] + 2.0 * padded[:, :, 1:-1] + padded[:, :, 2:]) * 0.25
    return (padded[:, :, :, :-2] + 2.0 * padded[:, :, :, 1:-1] + padded[:, :, :, 2:]) * 0.25

def upsample(coarse):
    return jnp.repeat(jnp.repeat(jnp.repeat(coarse, 4, axis=1), 4, axis=2), 4, axis=3)

def shift_weights(fine_offsets, fractions, axis_number):
    offset_k = fine_offsets[axis_number]
    frac_k = fractions[axis_number]
    weights = []
    for shift in range(-2, 3):
        lower = (offset_k == shift).astype(frac_k.dtype)
        upper = (offset_k + 1 == shift).astype(frac_k.dtype)
        weights.append((lower * (1.0 - frac_k) + upper * frac_k, upper - lower))
    return weights

def warp(moving_pad, fine_offsets, fractions):
    size_x, size_y, size_z = fine_offsets.shape[1:]
    weights_x = shift_weights(fine_offsets, fractions, 0)
    weights_y = shift_weights(fine_offsets, fractions, 1)
    weights_z = shift_weights(fine_offsets, fractions, 2)
    warped = None
    for index_x in range(5):
        wx, dx = weights_x[index_x]
        mid_w = None
        for index_y in range(5):
            wy, dy = weights_y[index_y]
            inner_w = None
            for index_z in range(5):
                wz, dz = weights_z[index_z]
                values = lax.slice(moving_pad, (index_x, index_y, index_z), (index_x + size_x, index_y + size_y, index_z + size_z))
                if inner_w is None:
                    inner_w = wz * values
                    inner_d = dz * values
                else:
                    inner_w = inner_w + wz * values
                    inner_d = inner_d + dz * values
            if mid_w is None:
                mid_w = wy * inner_w
                mid_dy = dy * inner_w
                mid_dz = wy * inner_d
            else:
                mid_w = mid_w + wy * inner_w
                mid_dy = mid_dy + dy * inner_w
                mid_dz = mid_dz + wy * inner_d
        if warped is None:
            warped = wx * mid_w
            slope_x = dx * mid_w
            slope_y = wx * mid_dy
            slope_z = wx * mid_dz
        else:
            warped = warped + wx * mid_w
            slope_x = slope_x + dx * mid_w
            slope_y = slope_y + wx * mid_dy
            slope_z = slope_z + wx * mid_dz
    return (warped, jnp.stack([slope_x, slope_y, slope_z]))

def box_axis(values, axis):
    length = values.shape[axis] - 8
    total = lax.slice_in_dim(values, 0, length, axis=axis)
    for start in range(1, 9):
        total = total + lax.slice_in_dim(values, start, start + length, axis=axis)
    return total

def box_sum(values):
    values = box_axis(values, values.ndim - 3)
    values = box_axis(values, values.ndim - 2)
    return box_axis(values, values.ndim - 1)

def lncc(fixed_ext, warped_ext):
    fields = jnp.stack([fixed_ext, warped_ext, fixed_ext * fixed_ext, warped_ext * warped_ext, fixed_ext * warped_ext])
    sums = box_sum(fields)
    fixed_sum, warped_sum = (sums[0], sums[1])
    cross = sums[4] - fixed_sum * warped_sum / window_count
    fixed_var = sums[2] - fixed_sum * fixed_sum / window_count
    warped_var = sums[3] - warped_sum * warped_sum / window_count
    denom = fixed_var * warped_var + epsilon
    similar = cross * cross / denom
    coef_a = 2.0 * cross / denom
    coef_b = -cross * cross * fixed_var / (denom * denom)
    coef_c = -(coef_a * fixed_sum + 2.0 * coef_b * warped_sum) / window_count
    return (similar, jnp.stack([coef_a, coef_b, coef_c]))

def restrict_grad(grad_warped, slopes, smoothed):
    grad_frac = grad_warped[None] * slopes
    chans, size_x, size_y, size_z = grad_frac.shape
    restricted = grad_frac.reshape(chans, size_x // 4, 4, size_y // 4, 4, size_z // 4, 4).sum(axis=(2, 4, 6))
    sigmoid_value = jax.nn.sigmoid(smoothed)
    return restricted * sigmoid_value * (1.0 - sigmoid_value)

def reference(fixed, moving, coarse_disp, offsets):
    smoothed = smooth_padded(jnp.pad(coarse_disp, ((0, 0), (1, 1), (1, 1), (1, 1))))
    fractions = upsample(jax.nn.sigmoid(smoothed))
    fine_offsets = upsample(offsets).astype(jnp.int32)
    warped, slopes = warp(jnp.pad(moving, 2), fine_offsets, fractions)
    similar, coeffs = lncc(jnp.pad(fixed, 4), jnp.pad(warped, 4))
    similarity = jnp.sum(similar) / jnp.float32(NX * NY * NZ)
    boxed = box_sum(jnp.pad(coeffs, ((0, 0), (4, 4), (4, 4), (4, 4))))
    grad_warped = -(fixed * boxed[0] + 2.0 * warped * boxed[1] + boxed[2])
    grad_smooth = restrict_grad(grad_warped, slopes, smoothed)
    grad_coarse = smooth_padded(jnp.pad(grad_smooth, ((0, 0), (1, 1), (1, 1), (1, 1))))
    return (similarity, grad_coarse)
```

```python
import functools
import jax
import jax.numpy as jnp
from jax import lax
from jax.experimental import pallas as pl
from jax.experimental.pallas import tpu as pltpu
from jax.sharding import PartitionSpec as P

window_count = 729.0
epsilon = 1e-05
MESH = pl.DeviceIdType.MESH
HIGHEST = lax.Precision.HIGHEST
PLANE = [(dx, dy) for dx in (-1, 0, 1) for dy in (-1, 0, 1) if (dx, dy) != (0, 0)]


def iota(shape, dim):
    return lax.broadcasted_iota(jnp.int32, shape, dim)


def dot(a, b):
    return jnp.dot(a, b, precision=HIGHEST, preferred_element_type=jnp.float32)


def as_float(mask):
    return jnp.where(mask, 1.0, 0.0).astype(jnp.float32)


def shifted(v, halo, s, lane):
    n = v.shape[-1]
    if s == 0:
        return v
    if s > 0:
        return pltpu.roll(jnp.where(lane < s, halo, v), n - s, v.ndim - 1)
    return pltpu.roll(jnp.where(lane >= n + s, halo, v), -s, v.ndim - 1)


def tent(diff):
    return jnp.where(diff == 0, 0.5, jnp.where(jnp.abs(diff) == 1, 0.25, 0.0))


def plane_filter():
    r = iota((16, 144), 0)
    c = iota((16, 144), 1)
    slot = c >> 4
    q = c & 15
    sx = jnp.where(slot >= 6, 2, jnp.where(slot >= 3, 1, 0))
    sy = slot - 3 * sx
    wx = tent(2 * sx + ((q >> 1) & 1) - 2 - ((r >> 1) & 1))
    wy = tent(2 * sy + (q & 1) - 2 - (r & 1))
    return jnp.where((r >> 2) == (q >> 2), wx * wy, 0.0).astype(jnp.float32)


def box_rows(v):
    s2 = v[:-1] + v[1:]
    s4 = s2[:-2] + s2[2:]
    s8 = s4[:-4] + s4[4:]
    return s8[:8] + v[8:16]


def kernel(sizes, count, fixed_ref, moving_ref, disp_ref, offs_ref, sim_ref, out_ref,
           cin, cup, cslot, gslot, gsrc, zc, zm, zf, zj, zk, zg, mext, fext, jext, cext, coef,
           shifts, slopes, smooth, offsets, tbox, tcoef, sims, send, recv):
    nx, ny, na = sizes
    me = {"gx": lax.axis_index("gx"), "gy": lax.axis_index("gy"), "ga": lax.axis_index("ga")}
    size = {"gx": nx, "gy": ny, "ga": na}
    pending = []
    counter = [0]

    def target(**moves):
        return {a: me[a] + moves.get(a, 0) for a in me}

    def exists(moves):
        conds = [((me[a] + d) >= 0) & ((me[a] + d) < size[a]) for a, d in moves.items() if d]
        return functools.reduce(jnp.logical_and, conds)

    def start(src, dst, moves):
        i = counter[0]
        counter[0] += 1
        c = pltpu.make_async_remote_copy(src, dst, send.at[i], recv.at[i],
                                         device_id=target(**moves), device_id_type=MESH)
        to = exists(moves)
        origin = exists({a: -d for a, d in moves.items()})
        pl.when(to)(c.start)
        pending.append((c, to))
        return c, origin

    def arrive(copies):
        for c, origin in copies:
            pl.when(origin)(c.wait_recv)

    def along(src, dst):
        return [start(src, dst.at[0], {"ga": 1}), start(src, dst.at[1], {"ga": -1})]

    def halo(z, lane):
        return jnp.where(lane < 64, z[1], z[0])

    def across(ext, lead, h):
        copies = []
        for dx, dy in PLANE:
            n = 8 if dx == 0 else h
            src0 = h + (8 - h if dx == 1 else 0)
            dst0 = {1: 0, 0: h, -1: h + 8}[dx]
            dsty = {1: 0, 0: 8, -1: 16}[dy]
            src = ext.at[lead, pl.ds(src0, n), pl.ds(8, 8), :]
            dst = ext.at[lead, pl.ds(dst0, n), pl.ds(dsty, 8), :]
            copies.append(start(src, dst, {"gx": dx, "gy": dy}))
        return copies

    def slots(ref):
        return [start(ref.at[4], ref.at[(1 - dx) * 3 + 1 - dy], {"gx": dx, "gy": dy}) for dx, dy in PLANE]

    def line(axis, base, tile):
        sims[base] = tile
        copies = []
        n = size[axis]
        for d in range(1, n):
            i = counter[0]
            counter[0] += 1
            dev = dict(me)
            dev[axis] = lax.rem(me[axis] + d, n)
            c = pltpu.make_async_remote_copy(sims.at[base], sims.at[base + d], send.at[i], recv.at[i],
                                             device_id=dev, device_id_type=MESH)
            c.start()
            pending.append((c, None))
            copies.append(c)
        return copies

    def line_sum(axis, base, copies):
        total = sims[base]
        for d, c in enumerate(copies):
            c.wait_recv()
            total = total + sims[base + 1 + d]
        return total

    for ref in (zc, zm, zf, zj, zk, zg, mext, fext, jext, cext, cslot, gslot, gsrc, cin):
        ref[...] = jnp.zeros(ref.shape, ref.dtype)

    barrier = pltpu.get_barrier_semaphore()
    expected = nx - 1 + ny - 1 + na - 1
    for axis in ("gx", "gy", "ga"):
        for d in range(1, size[axis]):
            dev = dict(me)
            dev[axis] = lax.rem(me[axis] + d, size[axis])
            pl.semaphore_signal(barrier, inc=1, device_id=dev, device_id_type=MESH)
    for dx, dy in PLANE:
        if dx and dy:
            moves = {"gx": dx, "gy": dy}
            cond = exists(moves)
            expected = expected + jnp.where(cond, 1, 0)

            def greet(moves=moves):
                pl.semaphore_signal(barrier, inc=1, device_id=target(**moves), device_id_type=MESH)

            pl.when(cond)(greet)

    for k in range(3):
        for cx in range(2):
            cin[0, pl.ds(4 * k + 2 * cx, 2), :] = disp_ref[k, cx]
            cin[1, pl.ds(4 * k + 2 * cx, 2), :] = offs_ref[k, cx].astype(jnp.float32)
    spread = as_float(iota((32, 128), 0) == (iota((32, 128), 1) >> 2))
    cup[0] = dot(cin[0], spread)
    offsets[...] = dot(cin[1], spread)
    mext[0, pl.ds(2, 8), pl.ds(8, 8), :] = moving_ref[...]
    fext[0, pl.ds(4, 8), pl.ds(8, 8), :] = fixed_ref[...]
    pl.semaphore_wait(barrier, expected)

    z_c = along(cup.at[0], zc)
    z_m = along(moving_ref, zm)
    m_center = across(mext, 0, 2)
    z_f = along(fixed_ref, zf)

    lane2 = iota((16, 128), 1)
    lane3 = iota((8, 8, 128), 2)
    arrive(z_c)
    u = cup[0]
    uh = halo(zc, lane2)
    cslot[4] = 0.25 * (shifted(u, uh, -4, lane2) + 2.0 * u + shifted(u, uh, 4, lane2))
    c_slots = slots(cslot)
    arrive(z_m)
    mext[1, pl.ds(2, 8), pl.ds(8, 8), :] = halo(zm, lane3)
    m_halo = across(mext, 1, 2)
    f_center = across(fext, 0, 4)
    arrive(z_f)
    fext[1, pl.ds(4, 8), pl.ds(8, 8), :] = halo(zf, lane3)
    f_halo = across(fext, 1, 4)

    filt = plane_filter()
    arrive(c_slots)
    smooth[...] = jax.nn.sigmoid(dot(filt, cslot[...].reshape(144, 128)))
    arrive(m_center)
    arrive(m_halo)
    lane_m = iota((12, 24, 128), 2)
    mv = mext[0]
    mh = mext[1]
    for iz in range(5):
        shifts[iz] = shifted(mv, mh, iz - 2, lane_m)

    low = iota((8, 128), 0) < 4

    def warp_row(r, carry):
        cx = r // 4
        weights = []
        for k in range(3):
            row = 4 * k + 2 * cx
            frac = jnp.where(low, smooth[pl.ds(row, 1), :], smooth[pl.ds(row + 1, 1), :])
            off = jnp.where(low, offsets[pl.ds(row, 1), :], offsets[pl.ds(row + 1, 1), :])
            pairs = []
            for shift in range(-2, 3):
                lower = off == float(shift)
                upper = off == float(shift - 1)
                w = jnp.where(lower, 1.0 - frac, jnp.where(upper, frac, 0.0))
                d = jnp.where(lower, -1.0, jnp.where(upper, 1.0, 0.0))
                pairs.append((w, d))
            weights.append(pairs)
        acc = None
        for ix in range(5):
            mid = None
            for iy in range(5):
                inner = None
                for iz in range(5):
                    v = shifts[iz, r + ix, pl.ds(6 + iy, 8), :]
                    wz, dz = weights[2][iz]
                    t = (wz * v, dz * v)
                    inner = t if inner is None else (inner[0] + t[0], inner[1] + t[1])
                wy, dy = weights[1][iy]
                t = (wy * inner[0], dy * inner[0], wy * inner[1])
                mid = t if mid is None else tuple(a + b for a, b in zip(mid, t))
            wx, dx = weights[0][ix]
            t = (wx * mid[0], dx * mid[0], wx * mid[1], wx * mid[2])
            acc = t if acc is None else tuple(a + b for a, b in zip(acc, t))
        jext[0, r + 4, pl.ds(8, 8), :] = acc[0]
        slopes[0, r] = acc[1]
        slopes[1, r] = acc[2]
        slopes[2, r] = acc[3]
        return carry

    lax.fori_loop(0, 8, warp_row, 0)

    z_j = along(jext.at[0, pl.ds(4, 8), pl.ds(8, 8), :], zj)
    j_center = across(jext, 0, 4)
    arrive(f_center)
    arrive(f_halo)
    for half in range(2):
        f = fext[half]
        tbox[0, half] = box_rows(f)
        tbox[2, half] = box_rows(f * f)
    arrive(z_j)
    jext[1, pl.ds(4, 8), pl.ds(8, 8), :] = halo(zj, lane3)
    j_halo = across(jext, 1, 4)
    zi = iota((256, 128), 0)
    zo = iota((256, 128), 1)
    band = as_float(((zi < 128) & (jnp.abs(zi - zo) <= 4))
                    | ((zi >= 128) & ((jnp.abs(zi - zo) <= 4) | (jnp.abs(zi - 256 - zo) <= 4))))

    def box_y(ref):
        total = ref[:, pl.ds(4, 8), :]
        for s in range(5, 13):
            total = total + ref[:, pl.ds(s, 8), :]
        return total

    arrive(j_center)
    arrive(j_halo)
    for half in range(2):
        f = fext[half]
        j = jext[half]
        tbox[1, half] = box_rows(j)
        tbox[3, half] = box_rows(j * j)
        tbox[4, half] = box_rows(f * j)
    sums = []
    for q in range(5):
        both = [box_y(tbox.at[q, half]).reshape(64, 128) for half in range(2)]
        sums.append(dot(jnp.concatenate(both, axis=1), band).reshape(8, 8, 128))
    fs, js = sums[0], sums[1]
    cross = sums[4] - fs * js / window_count
    fvar = sums[2] - fs * fs / window_count
    wvar = sums[3] - js * js / window_count
    den = fvar * wvar + epsilon
    inv = 1.0 / den
    ratio = cross * inv
    similar = cross * ratio
    ca = 2.0 * ratio
    cb = -(ratio * ratio) * fvar
    cc = -(ca * fs + 2.0 * cb * js) / window_count
    coef[0] = ca
    coef[1] = cb
    coef[2] = cc
    z_k = along(coef, zk)
    s_a = line("ga", 0, jnp.sum(similar, axis=0))
    arrive(z_k)
    for q in range(3):
        own = coef[q].reshape(64, 128)
        h = jnp.where(lane3 < 64, zk[1, q], zk[0, q]).reshape(64, 128)
        cext[q, pl.ds(4, 8), pl.ds(8, 8), :] = dot(jnp.concatenate([own, h], axis=1), band).reshape(8, 8, 128)
    c_copies = []
    for q in range(3):
        c_copies += across(cext, q, 4)
    s_x = line("gx", na, line_sum("ga", 0, s_a))
    arrive(c_copies)
    boxed = []
    for q in range(3):
        tcoef[q] = box_rows(cext[q])
    for q in range(3):
        boxed.append(box_y(tcoef.at[q]))
    grad = -(fixed_ref[...] * boxed[0] + 2.0 * jext[0, pl.ds(4, 8), pl.ds(8, 8), :] * boxed[1] + boxed[2])
    for k in range(3):
        t = grad * slopes[k]
        for cx in range(2):
            part = jnp.sum(t[4 * cx:4 * cx + 4], axis=0)
            for cy in range(2):
                row = jnp.sum(jnp.where(low == (cy == 0), part, 0.0), axis=0, keepdims=True)
                gsrc[pl.ds(4 * k + 2 * cx + cy, 1), :] = row
    group = as_float((iota((128, 128), 0) >> 2) == (iota((128, 128), 1) >> 2))
    s = smooth[...]
    u = dot(gsrc[...], group) * s * (1.0 - s)
    cup[1] = u
    z_g = along(cup.at[1], zg)
    s_y = line("gy", na + nx, line_sum("gx", na, s_x))
    arrive(z_g)
    uh = halo(zg, lane2)
    gslot[4] = 0.25 * (shifted(u, uh, -4, lane2) + 2.0 * u + shifted(u, uh, 4, lane2))
    g_slots = slots(gslot)
    total = line_sum("gy", na + nx, s_y)
    sim_ref[...] = (jnp.sum(total) / count).reshape(1, 1)
    arrive(g_slots)
    pick = as_float(iota((128, 32), 0) == (iota((128, 32), 1) << 2))
    final = dot(dot(filt, gslot[...].reshape(144, 128)), pick)
    for k in range(3):
        for cx in range(2):
            out_ref[k, cx] = final[4 * k + 2 * cx:4 * k + 2 * cx + 2]
    for c, to in pending:
        if to is None:
            c.wait_send()
        else:
            pl.when(to)(c.wait_send)


def solution(mesh):
    nx, ny, na = mesh.shape["gx"], mesh.shape["gy"], mesh.shape["ga"]

    def on_device(fixed, moving, disp, offs):
        count = float(fixed.size * nx * ny * na)
        f32 = jnp.float32
        vm = pltpu.VMEM
        copies = 160 + nx + ny + na
        sim, out = pl.pallas_call(
            functools.partial(kernel, (nx, ny, na), count),
            out_shape=(jax.ShapeDtypeStruct((1, 1), f32), jax.ShapeDtypeStruct(disp.shape, f32)),
            in_specs=[pl.BlockSpec(memory_space=pltpu.VMEM)] * 4,
            out_specs=(pl.BlockSpec(memory_space=pltpu.VMEM),) * 2,
            scratch_shapes=[
                vm((2, 16, 32), f32), vm((2, 16, 128), f32), vm((9, 16, 128), f32), vm((9, 16, 128), f32),
                vm((16, 128), f32), vm((2, 16, 128), f32), vm((2, 8, 8, 128), f32), vm((2, 8, 8, 128), f32),
                vm((2, 8, 8, 128), f32), vm((2, 3, 8, 8, 128), f32), vm((2, 16, 128), f32),
                vm((2, 12, 24, 128), f32), vm((2, 16, 24, 128), f32), vm((2, 16, 24, 128), f32),
                vm((3, 16, 24, 128), f32), vm((3, 8, 8, 128), f32), vm((5, 12, 24, 128), f32),
                vm((3, 8, 8, 128), f32), vm((16, 128), f32), vm((16, 128), f32),
                vm((5, 2, 8, 24, 128), f32), vm((3, 8, 24, 128), f32), vm((nx + ny + na, 8, 128), f32),
                pltpu.SemaphoreType.DMA((copies,)), pltpu.SemaphoreType.DMA((copies,)),
            ],
            compiler_params=pltpu.CompilerParams(
                collective_id=0, has_side_effects=True, vmem_limit_bytes=48 * 1024 * 1024),
        )(fixed, moving, disp, offs)
        return sim.reshape(()), out

    in_specs = (P("gx", "gy", "ga"), P("gx", "gy", "ga"), P(None, "gx", "gy", "ga"), P(None, "gx", "gy", "ga"))
    return jax.shard_map(on_device, mesh=mesh, in_specs=in_specs,
                         out_specs=(P(), P(None, "gx", "gy", "ga")), check_vma=False)
```

```python
import functools
import jax
import jax.numpy as jnp
from jax import lax
from jax.experimental import pallas as pl
from jax.experimental.pallas import tpu as pltpu
from jax.sharding import PartitionSpec as P

window_count = 729.0
epsilon = 1e-05
MESH = pl.DeviceIdType.MESH
HIGHEST = lax.Precision.HIGHEST
PLANE = [(dx, dy) for dx in (-1, 0, 1) for dy in (-1, 0, 1) if (dx, dy) != (0, 0)]


def iota(shape, dim):
    return lax.broadcasted_iota(jnp.int32, shape, dim)


def dot(a, b):
    return jnp.dot(a, b, precision=HIGHEST, preferred_element_type=jnp.float32)


def as_float(mask):
    return jnp.where(mask, 1.0, 0.0).astype(jnp.float32)


def shifted(v, halo, s, lane):
    n = v.shape[-1]
    if s == 0:
        return v
    if s > 0:
        return pltpu.roll(jnp.where(lane < s, halo, v), n - s, v.ndim - 1)
    return pltpu.roll(jnp.where(lane >= n + s, halo, v), -s, v.ndim - 1)


def tent(diff):
    return jnp.where(diff == 0, 0.5, jnp.where(jnp.abs(diff) == 1, 0.25, 0.0))


def plane_filter():
    r = iota((16, 144), 0)
    c = iota((16, 144), 1)
    slot = c >> 4
    q = c & 15
    sx = jnp.where(slot >= 6, 2, jnp.where(slot >= 3, 1, 0))
    sy = slot - 3 * sx
    wx = tent(2 * sx + ((q >> 1) & 1) - 2 - ((r >> 1) & 1))
    wy = tent(2 * sy + (q & 1) - 2 - (r & 1))
    return jnp.where((r >> 2) == (q >> 2), wx * wy, 0.0).astype(jnp.float32)


def box_rows(v):
    s2 = v[:-1] + v[1:]
    s4 = s2[:-2] + s2[2:]
    s8 = s4[:-4] + s4[4:]
    return s8[:8] + v[8:16]


def kernel(sizes, count, fixed_ref, moving_ref, disp_ref, offs_ref, sim_ref, out_ref,
           cin, cup, cslot, gslot, gsrc, zc, zg, edge, zedge, qi, qj, hm, hf, hj, hk, mext, fext, jext, cext, coef,
           shifts, slopes, smooth, offsets, tbox, tcoef, sims, send, recv):
    nx, ny, na = sizes
    me = {"gx": lax.axis_index("gx"), "gy": lax.axis_index("gy"), "ga": lax.axis_index("ga")}
    size = {"gx": nx, "gy": ny, "ga": na}
    pending = []
    counter = [0]

    def target(**moves):
        return {a: me[a] + moves.get(a, 0) for a in me}

    def exists(moves):
        conds = [((me[a] + d) >= 0) & ((me[a] + d) < size[a]) for a, d in moves.items() if d]
        return functools.reduce(jnp.logical_and, conds)

    def start(src, dst, moves):
        i = counter[0]
        counter[0] += 1
        c = pltpu.make_async_remote_copy(src, dst, send.at[i], recv.at[i],
                                         device_id=target(**moves), device_id_type=MESH)
        to = exists(moves)
        origin = exists({a: -d for a, d in moves.items()})
        pl.when(to)(c.start)
        pending.append((c, to))
        return c, origin

    def arrive(copies):
        for c, origin in copies:
            pl.when(origin)(c.wait_recv)

    def along(src, dst):
        return [start(src, dst.at[0], {"ga": 1}), start(src, dst.at[1], {"ga": -1})]

    def halo(z, lane):
        return jnp.where(lane < 64, z[1], z[0])

    def across(ext, lead, h):
        copies = []
        for dx, dy in PLANE:
            n = 8 if dx == 0 else h
            src0 = h + (8 - h if dx == 1 else 0)
            dst0 = {1: 0, 0: h, -1: h + 8}[dx]
            wide = 8 if dy == 0 else 4
            srcy = 12 if dy == 1 else 8
            dsty = {1: 4, 0: 8, -1: 16}[dy]
            src = ext.at[lead, pl.ds(src0, n), pl.ds(srcy, wide), :]
            dst = ext.at[lead, pl.ds(dst0, n), pl.ds(dsty, wide), :]
            copies.append(start(src, dst, {"gx": dx, "gy": dy}))
        return copies

    def slots(ref):
        return [start(ref.at[4], ref.at[(1 - dx) * 3 + 1 - dy], {"gx": dx, "gy": dy}) for dx, dy in PLANE]

    def line(axis, base, tile):
        sims[base] = tile
        copies = []
        n = size[axis]
        for d in range(1, n):
            i = counter[0]
            counter[0] += 1
            dev = dict(me)
            dev[axis] = lax.rem(me[axis] + d, n)
            c = pltpu.make_async_remote_copy(sims.at[base], sims.at[base + d], send.at[i], recv.at[i],
                                             device_id=dev, device_id_type=MESH)
            c.start()
            pending.append((c, None))
            copies.append(c)
        return copies

    def line_sum(axis, base, copies):
        total = sims[base]
        for d, c in enumerate(copies):
            c.wait_recv()
            total = total + sims[base + 1 + d]
        return total

    lane1 = iota((8, 128), 1)

    def pack(rows):
        tile = jnp.zeros((8, 128), jnp.float32)
        for i, v in enumerate(rows):
            tile = jnp.where((lane1 >> 3) == i, pltpu.roll(v, (4 + 8 * i) % 128, 1), tile)
        return tile

    def merged(i):
        return jnp.where((lane1 & 7) < 4, zedge[i, 0], zedge[i, 1])

    def unpack(tile, i):
        return pltpu.roll(tile, (124 - 8 * i) % 128, 1)

    def halo_rows(ref, q, h, first):
        for sy in range(3):
            for sx, x0, n, d0 in ((0, 8 - h, h, 0), (1, 0, 8, h), (2, 0, h, h + 8)):
                tile = q[3 * sx + sy]
                for x in range(n):
                    ref[d0 + x, pl.ds(8 * sy, 8), :] = unpack(tile, first + x0 + x)

    for ref in (zc, zg, zedge, qi, qj, mext, fext, jext, cext, cslot, gslot, gsrc, cin):
        ref[...] = jnp.zeros(ref.shape, ref.dtype)

    barrier = pltpu.get_barrier_semaphore()
    expected = nx - 1 + ny - 1 + na - 1
    for axis in ("gx", "gy", "ga"):
        for d in range(1, size[axis]):
            dev = dict(me)
            dev[axis] = lax.rem(me[axis] + d, size[axis])
            pl.semaphore_signal(barrier, inc=1, device_id=dev, device_id_type=MESH)
    for dx, dy in PLANE:
        if dx and dy:
            moves = {"gx": dx, "gy": dy}
            cond = exists(moves)
            expected = expected + jnp.where(cond, 1, 0)

            def greet(moves=moves):
                pl.semaphore_signal(barrier, inc=1, device_id=target(**moves), device_id_type=MESH)

            pl.when(cond)(greet)

    for k in range(3):
        for cx in range(2):
            cin[0, pl.ds(4 * k + 2 * cx, 2), :] = disp_ref[k, cx]
            cin[1, pl.ds(4 * k + 2 * cx, 2), :] = offs_ref[k, cx].astype(jnp.float32)
    spread = as_float(iota((32, 128), 0) == (iota((32, 128), 1) >> 2))
    cup[0] = dot(cin[0], spread)
    offsets[...] = dot(cin[1], spread)
    mext[0, pl.ds(2, 8), pl.ds(8, 8), :] = moving_ref[...]
    edge[0] = pack([moving_ref[i] for i in range(8)] + [fixed_ref[i] for i in range(8)])
    fext[0, pl.ds(4, 8), pl.ds(8, 8), :] = fixed_ref[...]
    pl.semaphore_wait(barrier, expected)

    z_c = along(cup.at[0], zc)
    z_i = along(edge.at[0], zedge.at[0])
    m_center = across(mext, 0, 2)
    f_center = across(fext, 0, 4)

    lane2 = iota((16, 128), 1)
    arrive(z_c)
    u = cup[0]
    uh = halo(zc, lane2)
    cslot[4] = 0.25 * (shifted(u, uh, -4, lane2) + 2.0 * u + shifted(u, uh, 4, lane2))
    c_slots = slots(cslot)
    arrive(z_i)
    qi[4] = merged(0)
    i_slots = slots(qi)

    filt = plane_filter()
    arrive(c_slots)
    smooth[...] = jax.nn.sigmoid(dot(filt, cslot[...].reshape(144, 128)))
    arrive(i_slots)
    halo_rows(hm, qi, 2, 0)
    arrive(m_center)
    lane_m = iota((12, 24, 128), 2)
    mv = mext[0]
    mh = hm[...]
    for iz in range(5):
        shifts[iz] = shifted(mv, mh, iz - 2, lane_m)

    low = iota((8, 128), 0) < 4

    def warp_row(r, carry):
        cx = r // 4
        weights = []
        for k in range(3):
            row = 4 * k + 2 * cx
            frac = jnp.where(low, smooth[pl.ds(row, 1), :], smooth[pl.ds(row + 1, 1), :])
            off = jnp.where(low, offsets[pl.ds(row, 1), :], offsets[pl.ds(row + 1, 1), :])
            pairs = []
            for shift in range(-2, 3):
                lower = off == float(shift)
                upper = off == float(shift - 1)
                w = jnp.where(lower, 1.0 - frac, jnp.where(upper, frac, 0.0))
                d = jnp.where(lower, -1.0, jnp.where(upper, 1.0, 0.0))
                pairs.append((w, d))
            weights.append(pairs)
        acc = None
        for ix in range(5):
            mid = None
            for iy in range(5):
                inner = None
                for iz in range(5):
                    v = shifts[iz, r + ix, pl.ds(6 + iy, 8), :]
                    wz, dz = weights[2][iz]
                    t = (wz * v, dz * v)
                    inner = t if inner is None else (inner[0] + t[0], inner[1] + t[1])
                wy, dy = weights[1][iy]
                t = (wy * inner[0], dy * inner[0], wy * inner[1])
                mid = t if mid is None else tuple(a + b for a, b in zip(mid, t))
            wx, dx = weights[0][ix]
            t = (wx * mid[0], dx * mid[0], wx * mid[1], wx * mid[2])
            acc = t if acc is None else tuple(a + b for a, b in zip(acc, t))
        jext[0, r + 4, pl.ds(8, 8), :] = acc[0]
        slopes[0, r] = acc[1]
        slopes[1, r] = acc[2]
        slopes[2, r] = acc[3]
        return carry

    lax.fori_loop(0, 8, warp_row, 0)

    edge[1] = pack([jext[0, 4 + i, pl.ds(8, 8), :] for i in range(8)])
    z_j = along(edge.at[1], zedge.at[1])
    j_center = across(jext, 0, 4)
    arrive(z_j)
    qj[4] = merged(1)
    j_slots = slots(qj)
    halo_rows(hf, qi, 4, 8)
    arrive(f_center)
    for half in range(2):
        f = (fext[0], hf[...])[half]
        tbox[0, half] = box_rows(f)
        tbox[2, half] = box_rows(f * f)
    zi = iota((256, 128), 0)
    zo = iota((256, 128), 1)
    band = as_float(((zi < 128) & (jnp.abs(zi - zo) <= 4))
                    | ((zi >= 128) & ((jnp.abs(zi - zo) <= 4) | (jnp.abs(zi - 256 - zo) <= 4))))

    def box_y(ref):
        total = ref[:, pl.ds(4, 8), :]
        for s in range(5, 13):
            total = total + ref[:, pl.ds(s, 8), :]
        return total

    arrive(j_slots)
    halo_rows(hj, qj, 4, 0)
    arrive(j_center)
    for half in range(2):
        f = (fext[0], hf[...])[half]
        j = (jext[0], hj[...])[half]
        tbox[1, half] = box_rows(j)
        tbox[3, half] = box_rows(j * j)
        tbox[4, half] = box_rows(f * j)
    sums = []
    for q in range(5):
        both = [box_y(tbox.at[q, half]).reshape(64, 128) for half in range(2)]
        sums.append(dot(jnp.concatenate(both, axis=1), band).reshape(8, 8, 128))
    fs, js = sums[0], sums[1]
    cross = sums[4] - fs * js / window_count
    fvar = sums[2] - fs * fs / window_count
    wvar = sums[3] - js * js / window_count
    den = fvar * wvar + epsilon
    inv = 1.0 / den
    ratio = cross * inv
    similar = cross * ratio
    ca = 2.0 * ratio
    cb = -(ratio * ratio) * fvar
    cc = -(ca * fs + 2.0 * cb * js) / window_count
    coef[0] = ca
    coef[1] = cb
    coef[2] = cc
    rows = [ca[i] for i in range(8)] + [cb[i] for i in range(8)]
    edge[2] = pack(rows)
    edge[3] = pack([cc[i] for i in range(8)])
    z_k = along(edge.at[2], zedge.at[2]) + along(edge.at[3], zedge.at[3])
    s_a = line("ga", 0, jnp.sum(similar, axis=0))
    arrive(z_k)
    for q in range(3):
        own = coef[q].reshape(64, 128)
        tile = merged(2 + q // 2)
        for x in range(8):
            hk[x] = unpack(tile, 8 * (q % 2) + x)
        h = hk[...].reshape(64, 128)
        cext[q, pl.ds(4, 8), pl.ds(8, 8), :] = dot(jnp.concatenate([own, h], axis=1), band).reshape(8, 8, 128)
    c_copies = []
    for q in range(3):
        c_copies += across(cext, q, 4)
    s_x = line("gx", na, line_sum("ga", 0, s_a))
    arrive(c_copies)
    boxed = []
    for q in range(3):
        tcoef[q] = box_rows(cext[q])
    for q in range(3):
        boxed.append(box_y(tcoef.at[q]))
    grad = -(fixed_ref[...] * boxed[0] + 2.0 * jext[0, pl.ds(4, 8), pl.ds(8, 8), :] * boxed[1] + boxed[2])
    for k in range(3):
        t = grad * slopes[k]
        for cx in range(2):
            part = jnp.sum(t[4 * cx:4 * cx + 4], axis=0)
            for cy in range(2):
                row = jnp.sum(jnp.where(low == (cy == 0), part, 0.0), axis=0, keepdims=True)
                gsrc[pl.ds(4 * k + 2 * cx + cy, 1), :] = row
    group = as_float((iota((128, 128), 0) >> 2) == (iota((128, 128), 1) >> 2))
    s = smooth[...]
    u = dot(gsrc[...], group) * s * (1.0 - s)
    cup[1] = u
    z_g = along(cup.at[1], zg)
    s_y = line("gy", na + nx, line_sum("gx", na, s_x))
    arrive(z_g)
    uh = halo(zg, lane2)
    gslot[4] = 0.25 * (shifted(u, uh, -4, lane2) + 2.0 * u + shifted(u, uh, 4, lane2))
    g_slots = slots(gslot)
    total = line_sum("gy", na + nx, s_y)
    sim_ref[...] = (jnp.sum(total) / count).reshape(1, 1)
    arrive(g_slots)
    pick = as_float(iota((128, 32), 0) == (iota((128, 32), 1) << 2))
    final = dot(dot(filt, gslot[...].reshape(144, 128)), pick)
    for k in range(3):
        for cx in range(2):
            out_ref[k, cx] = final[4 * k + 2 * cx:4 * k + 2 * cx + 2]
    for c, to in pending:
        if to is None:
            c.wait_send()
        else:
            pl.when(to)(c.wait_send)


def solution(mesh):
    nx, ny, na = mesh.shape["gx"], mesh.shape["gy"], mesh.shape["ga"]

    def on_device(fixed, moving, disp, offs):
        count = float(fixed.size * nx * ny * na)
        f32 = jnp.float32
        vm = pltpu.VMEM
        copies = 160 + nx + ny + na
        sim, out = pl.pallas_call(
            functools.partial(kernel, (nx, ny, na), count),
            out_shape=(jax.ShapeDtypeStruct((1, 1), f32), jax.ShapeDtypeStruct(disp.shape, f32)),
            in_specs=[pl.BlockSpec(memory_space=pltpu.VMEM)] * 4,
            out_specs=(pl.BlockSpec(memory_space=pltpu.VMEM),) * 2,
            scratch_shapes=[
                vm((2, 16, 32), f32), vm((2, 16, 128), f32), vm((9, 16, 128), f32), vm((9, 16, 128), f32),
                vm((16, 128), f32), vm((2, 16, 128), f32), vm((2, 16, 128), f32),
                vm((4, 8, 128), f32), vm((4, 2, 8, 128), f32), vm((9, 8, 128), f32), vm((9, 8, 128), f32),
                vm((12, 24, 128), f32), vm((16, 24, 128), f32), vm((16, 24, 128), f32), vm((8, 8, 128), f32),
                vm((1, 12, 24, 128), f32), vm((1, 16, 24, 128), f32), vm((1, 16, 24, 128), f32),
                vm((3, 16, 24, 128), f32), vm((3, 8, 8, 128), f32), vm((5, 12, 24, 128), f32),
                vm((3, 8, 8, 128), f32), vm((16, 128), f32), vm((16, 128), f32),
                vm((5, 2, 8, 24, 128), f32), vm((3, 8, 24, 128), f32), vm((nx + ny + na, 8, 128), f32),
                pltpu.SemaphoreType.DMA((copies,)), pltpu.SemaphoreType.DMA((copies,)),
            ],
            compiler_params=pltpu.CompilerParams(
                collective_id=0, has_side_effects=True, vmem_limit_bytes=48 * 1024 * 1024),
        )(fixed, moving, disp, offs)
        return sim.reshape(()), out

    in_specs = (P("gx", "gy", "ga"), P("gx", "gy", "ga"), P(None, "gx", "gy", "ga"), P(None, "gx", "gy", "ga"))
    return jax.shard_map(on_device, mesh=mesh, in_specs=in_specs,
                         out_specs=(P(), P(None, "gx", "gy", "ga")), check_vma=False)
```

```python
import functools
import jax
import jax.numpy as jnp
from jax import lax
from jax.experimental import pallas as pl
from jax.experimental.pallas import tpu as pltpu
from jax.sharding import PartitionSpec as P

window_count = 729.0
epsilon = 1e-05
MESH = pl.DeviceIdType.MESH
HIGHEST = lax.Precision.HIGHEST
NINE = [(dx, dy) for dx in (0, -1, 1) for dy in (0, -1, 1)]
PLANE = [(dx, dy) for dx in (-1, 0, 1) for dy in (-1, 0, 1) if (dx, dy) != (0, 0)]


def iota(shape, dim):
    return lax.broadcasted_iota(jnp.int32, shape, dim)


def dot(a, b):
    return jnp.dot(a, b, precision=HIGHEST, preferred_element_type=jnp.float32)


def as_float(mask):
    return jnp.where(mask, 1.0, 0.0).astype(jnp.float32)


def shifted(v, halo, s, lane):
    n = v.shape[-1]
    if s == 0:
        return v
    if s > 0:
        return pltpu.roll(jnp.where(lane < s, halo, v), n - s, v.ndim - 1)
    return pltpu.roll(jnp.where(lane >= n + s, halo, v), -s, v.ndim - 1)


def tent(diff):
    return jnp.where(diff == 0, 0.5, jnp.where(jnp.abs(diff) == 1, 0.25, 0.0))


def plane_filter():
    r = iota((16, 144), 0)
    c = iota((16, 144), 1)
    slot = c >> 4
    q = c & 15
    sx = jnp.where(slot >= 6, 2, jnp.where(slot >= 3, 1, 0))
    sy = slot - 3 * sx
    wx = tent(2 * sx + ((q >> 1) & 1) - 2 - ((r >> 1) & 1))
    wy = tent(2 * sy + (q & 1) - 2 - (r & 1))
    return jnp.where((r >> 2) == (q >> 2), wx * wy, 0.0).astype(jnp.float32)


def box_rows(v):
    s2 = v[:-1] + v[1:]
    s4 = s2[:-2] + s2[2:]
    s8 = s4[:-4] + s4[4:]
    return s8[:8] + v[8:16]


def kernel(sizes, count, fixed_any, moving_any, disp_any, offs_any, sim_ref, out_ref,
           fixed_ref, moving_ref, disp_ref, offs_ref, local,
           cin, cslot, gslot, gsrc, edge_i, edge_j, edge_k, edge_g, zi_, zj_, zk_, zg_, hm, hf, hj, hk, mext, fext, jext, cext,
           shifts, slopes, smooth, offsets, tbox, tcoef, sims, send, recv):
    nx, ny, na = sizes
    me = {"gx": lax.axis_index("gx"), "gy": lax.axis_index("gy"), "ga": lax.axis_index("ga")}
    size = {"gx": nx, "gy": ny, "ga": na}
    pending = []
    counter = [0]

    def target(**moves):
        return {a: me[a] + moves.get(a, 0) for a in me}

    def exists(moves):
        conds = [((me[a] + d) >= 0) & ((me[a] + d) < size[a]) for a, d in moves.items() if d]
        return functools.reduce(jnp.logical_and, conds)

    def start(src, dst, moves):
        i = counter[0]
        counter[0] += 1
        c = pltpu.make_async_remote_copy(src, dst, send.at[i], recv.at[i],
                                         device_id=target(**moves), device_id_type=MESH)
        to = exists(moves)
        origin = exists({a: -d for a, d in moves.items()})
        pl.when(to)(c.start)
        pending.append((c, to))
        return c, origin

    def arrive(copies):
        for c, origin in copies:
            pl.when(origin)(c.wait_recv)

    def along(src, dst):
        return [start(src, dst.at[i, (1 - dx) * 3 + 1 - dy], {"gx": dx, "gy": dy, "ga": dz})
                for dx, dy in NINE for i, dz in ((0, 1), (1, -1))]

    def across(ext, lead, h):
        copies = []
        for dx, dy in PLANE:
            n = 8 if dx == 0 else h
            src0 = h + (8 - h if dx == 1 else 0)
            dst0 = {1: 0, 0: h, -1: h + 8}[dx]
            wide = 8 if dy == 0 else 4
            srcy = 12 if dy == 1 else 8
            dsty = {1: 4, 0: 8, -1: 16}[dy]
            src = ext.at[lead, pl.ds(src0, n), pl.ds(srcy, wide), :]
            dst = ext.at[lead, pl.ds(dst0, n), pl.ds(dsty, wide), :]
            copies.append(start(src, dst, {"gx": dx, "gy": dy}))
        return copies

    def slots(ref):
        return [start(ref.at[4], ref.at[(1 - dx) * 3 + 1 - dy], {"gx": dx, "gy": dy}) for dx, dy in PLANE]

    def line(axis, base, tile):
        sims[base] = tile
        copies = []
        n = size[axis]
        for d in range(1, n):
            i = counter[0]
            counter[0] += 1
            dev = dict(me)
            dev[axis] = lax.rem(me[axis] + d, n)
            c = pltpu.make_async_remote_copy(sims.at[base], sims.at[base + d], send.at[i], recv.at[i],
                                             device_id=dev, device_id_type=MESH)
            c.start()
            pending.append((c, None))
            copies.append(c)
        return copies

    def line_sum(axis, base, copies):
        total = sims[base]
        for d, c in enumerate(copies):
            c.wait_recv()
            total = total + sims[base + 1 + d]
        return total

    lane1 = iota((8, 128), 1)

    def pack(rows):
        tile = jnp.zeros((8, 128), jnp.float32)
        for i, v in enumerate(rows):
            tile = jnp.where((lane1 >> 3) == i, pltpu.roll(v, (4 + 8 * i) % 128, 1), tile)
        return tile

    def merged(i):
        z, part = i
        if part is None:
            return lambda q: jnp.where((lane1 & 7) < 4, z[0, q], z[1, q])
        return lambda q: jnp.where((lane1 & 7) < 4, z[0, q, part], z[1, q, part])

    def unpack(tile, i):
        return pltpu.roll(tile, (124 - 8 * i) % 128, 1)

    def halo_rows(ref, q, h, first):
        for sy in range(3):
            for sx, x0, n, d0 in ((0, 8 - h, h, 0), (1, 0, 8, h), (2, 0, h, h + 8)):
                tile = q(3 * sx + sy)
                for x in range(n):
                    ref[d0 + x, pl.ds(8 * sy, 8), :] = unpack(tile, first + x0 + x)

    def smooth_z(slots_ref, q):
        rows = []
        for slot in range(9):
            tile = q(slot)
            u = slots_ref[slot]
            uh = jnp.concatenate([unpack(tile, 0), unpack(tile, 1)], axis=0)
            rows.append(0.25 * (shifted(u, uh, -4, lane2) + 2.0 * u + shifted(u, uh, 4, lane2)))
        return jnp.concatenate(rows, axis=0)

    loads = [pltpu.make_async_copy(a, b, local.at[i]) for i, (a, b) in enumerate(
        ((disp_any, disp_ref), (offs_any, offs_ref), (moving_any, moving_ref), (fixed_any, fixed_ref)))]
    for c in loads:
        c.start()
    lane2 = iota((16, 128), 1)

    for ref in (zi_, zj_, zk_, zg_, mext, fext, jext, cext, cslot, gslot, gsrc, cin):
        ref[...] = jnp.zeros(ref.shape, ref.dtype)

    barrier = pltpu.get_barrier_semaphore()
    expected = nx - 1 + ny - 1 + na - 1
    for axis in ("gx", "gy", "ga"):
        for d in range(1, size[axis]):
            dev = dict(me)
            dev[axis] = lax.rem(me[axis] + d, size[axis])
            pl.semaphore_signal(barrier, inc=1, device_id=dev, device_id_type=MESH)
    for dx, dy in NINE:
        for dz in (-1, 0, 1):
            if (dx != 0) + (dy != 0) + (dz != 0) < 2:
                continue
            moves = {"gx": dx, "gy": dy, "ga": dz}
            cond = exists(moves)
            expected = expected + jnp.where(cond, 1, 0)

            def greet(moves=moves):
                pl.semaphore_signal(barrier, inc=1, device_id=target(**moves), device_id_type=MESH)

            pl.when(cond)(greet)

    for c in loads:
        c.wait()
    for k in range(3):
        for cx in range(2):
            cin[0, pl.ds(4 * k + 2 * cx, 2), :] = disp_ref[k, cx]
            cin[1, pl.ds(4 * k + 2 * cx, 2), :] = offs_ref[k, cx].astype(jnp.float32)
    spread = as_float(iota((32, 128), 0) == (iota((32, 128), 1) >> 2))
    cslot[4] = dot(cin[0], spread)
    offsets[...] = dot(cin[1], spread)
    mext[0, pl.ds(2, 8), pl.ds(8, 8), :] = moving_ref[...]
    edge_i[1] = pack([cslot[4, 0:8], cslot[4, 8:16]])
    edge_i[0] = pack([moving_ref[i] for i in range(8)] + [fixed_ref[i] for i in range(8)])
    fext[0, pl.ds(4, 8), pl.ds(8, 8), :] = fixed_ref[...]
    pl.semaphore_wait(barrier, expected)

    z_i = along(edge_i, zi_)
    c_slots = slots(cslot)
    m_center = across(mext, 0, 2)
    f_center = across(fext, 0, 4)
    filt = plane_filter()
    arrive(c_slots)
    arrive(z_i)
    smooth[...] = jax.nn.sigmoid(dot(filt, smooth_z(cslot, merged((zi_, 1)))))
    halo_rows(hm, merged((zi_, 0)), 2, 0)
    arrive(m_center)
    lane_m = iota((12, 24, 128), 2)
    mv = mext[0]
    mh = hm[...]
    for iz in range(5):
        shifts[iz] = shifted(mv, mh, iz - 2, lane_m)

    low = iota((8, 128), 0) < 4

    def warp_row(r, carry):
        cx = r // 4
        weights = []
        for k in range(3):
            row = 4 * k + 2 * cx
            frac = jnp.where(low, smooth[pl.ds(row, 1), :], smooth[pl.ds(row + 1, 1), :])
            off = jnp.where(low, offsets[pl.ds(row, 1), :], offsets[pl.ds(row + 1, 1), :])
            pairs = []
            for shift in range(-2, 3):
                lower = off == float(shift)
                upper = off == float(shift - 1)
                w = jnp.where(lower, 1.0 - frac, jnp.where(upper, frac, 0.0))
                d = jnp.where(lower, -1.0, jnp.where(upper, 1.0, 0.0))
                pairs.append((w, d))
            weights.append(pairs)
        acc = None
        for ix in range(5):
            mid = None
            for iy in range(5):
                inner = None
                for iz in range(5):
                    v = shifts[iz, r + ix, pl.ds(6 + iy, 8), :]
                    wz, dz = weights[2][iz]
                    t = (wz * v, dz * v)
                    inner = t if inner is None else (inner[0] + t[0], inner[1] + t[1])
                wy, dy = weights[1][iy]
                t = (wy * inner[0], dy * inner[0], wy * inner[1])
                mid = t if mid is None else tuple(a + b for a, b in zip(mid, t))
            wx, dx = weights[0][ix]
            t = (wx * mid[0], dx * mid[0], wx * mid[1], wx * mid[2])
            acc = t if acc is None else tuple(a + b for a, b in zip(acc, t))
        jext[0, r + 4, pl.ds(8, 8), :] = acc[0]
        slopes[0, r] = acc[1]
        slopes[1, r] = acc[2]
        slopes[2, r] = acc[3]
        return carry

    lax.fori_loop(0, 8, warp_row, 0)

    edge_j[...] = pack([jext[0, 4 + i, pl.ds(8, 8), :] for i in range(8)])
    z_j = along(edge_j, zj_)
    j_center = across(jext, 0, 4)
    halo_rows(hf, merged((zi_, 0)), 4, 8)
    arrive(f_center)
    for half in range(2):
        f = (fext[0], hf[...])[half]
        tbox[0, half] = box_rows(f)
        tbox[2, half] = box_rows(f * f)
    zi = iota((256, 128), 0)
    zo = iota((256, 128), 1)
    band = as_float(((zi < 128) & (jnp.abs(zi - zo) <= 4))
                    | ((zi >= 128) & ((jnp.abs(zi - zo) <= 4) | (jnp.abs(zi - 256 - zo) <= 4))))

    def box_y(ref):
        total = ref[:, pl.ds(4, 8), :]
        for s in range(5, 13):
            total = total + ref[:, pl.ds(s, 8), :]
        return total

    arrive(z_j)
    halo_rows(hj, merged((zj_, None)), 4, 0)
    arrive(j_center)
    for half in range(2):
        f = (fext[0], hf[...])[half]
        j = (jext[0], hj[...])[half]
        tbox[1, half] = box_rows(j)
        tbox[3, half] = box_rows(j * j)
        tbox[4, half] = box_rows(f * j)
    sums = []
    for q in range(5):
        both = [box_y(tbox.at[q, half]).reshape(64, 128) for half in range(2)]
        sums.append(dot(jnp.concatenate(both, axis=1), band).reshape(8, 8, 128))
    fs, js = sums[0], sums[1]
    cross = sums[4] - fs * js / window_count
    fvar = sums[2] - fs * fs / window_count
    wvar = sums[3] - js * js / window_count
    den = fvar * wvar + epsilon
    inv = 1.0 / den
    ratio = cross * inv
    similar = cross * ratio
    ca = 2.0 * ratio
    cb = -(ratio * ratio) * fvar
    cc = -(ca * fs + 2.0 * cb * js) / window_count
    rows = [ca[i] for i in range(8)] + [cb[i] for i in range(8)]
    edge_k[0] = pack(rows)
    edge_k[1] = pack([cc[i] for i in range(8)])
    z_k = along(edge_k, zk_)
    c_copies = []
    for q, v in enumerate((ca, cb, cc)):
        cext[q, pl.ds(4, 8), pl.ds(8, 8), :] = v
        c_copies += across(cext, q, 4)
    s_a = line("ga", 0, jnp.sum(similar, axis=0))
    s_x = line("gx", na, line_sum("ga", 0, s_a))
    arrive(z_k)
    for q in range(3):
        halo_rows(hk.at[q], merged((zk_, q // 2)), 4, 8 * (q % 2))
        tcoef[q, 1] = box_rows(hk[q])
    arrive(c_copies)
    boxed = []
    for q in range(3):
        tcoef[q, 0] = box_rows(cext[q])
    for q in range(3):
        both = [box_y(tcoef.at[q, half]).reshape(64, 128) for half in range(2)]
        boxed.append(dot(jnp.concatenate(both, axis=1), band).reshape(8, 8, 128))
    grad = -(fixed_ref[...] * boxed[0] + 2.0 * jext[0, pl.ds(4, 8), pl.ds(8, 8), :] * boxed[1] + boxed[2])
    for k in range(3):
        t = grad * slopes[k]
        for cx in range(2):
            part = jnp.sum(t[4 * cx:4 * cx + 4], axis=0)
            for cy in range(2):
                row = jnp.sum(jnp.where(low == (cy == 0), part, 0.0), axis=0, keepdims=True)
                gsrc[pl.ds(4 * k + 2 * cx + cy, 1), :] = row
    group = as_float((iota((128, 128), 0) >> 2) == (iota((128, 128), 1) >> 2))
    s = smooth[...]
    u = dot(gsrc[...], group) * s * (1.0 - s)
    gslot[4] = u
    edge_g[...] = pack([u[:8], u[8:]])
    z_g = along(edge_g, zg_)
    g_slots = slots(gslot)
    s_y = line("gy", na + nx, line_sum("gx", na, s_x))
    total = line_sum("gy", na + nx, s_y)
    sim_ref[...] = (jnp.sum(total) / count).reshape(1, 1)
    arrive(g_slots)
    arrive(z_g)
    pick = as_float(iota((128, 32), 0) == (iota((128, 32), 1) << 2))
    final = dot(dot(filt, smooth_z(gslot, merged((zg_, None)))), pick)
    for k in range(3):
        for cx in range(2):
            out_ref[k, cx] = final[4 * k + 2 * cx:4 * k + 2 * cx + 2]
    for c, to in pending:
        if to is None:
            c.wait_send()
        else:
            pl.when(to)(c.wait_send)


def solution(mesh):
    nx, ny, na = mesh.shape["gx"], mesh.shape["gy"], mesh.shape["ga"]

    def on_device(fixed, moving, disp, offs):
        count = float(fixed.size * nx * ny * na)
        f32 = jnp.float32
        vm = pltpu.VMEM
        copies = 192 + nx + ny + na
        sim, out = pl.pallas_call(
            functools.partial(kernel, (nx, ny, na), count),
            out_shape=(jax.ShapeDtypeStruct((1, 1), f32), jax.ShapeDtypeStruct(disp.shape, f32)),
            in_specs=[pl.BlockSpec(memory_space=pltpu.HBM)] * 4,
            out_specs=(pl.BlockSpec(memory_space=pltpu.VMEM),) * 2,
            scratch_shapes=[
                vm(fixed.shape, f32), vm(moving.shape, f32), vm(disp.shape, f32), vm(offs.shape, jnp.int32),
                pltpu.SemaphoreType.DMA((4,)),
                vm((2, 16, 32), f32), vm((9, 16, 128), f32), vm((9, 16, 128), f32), vm((16, 128), f32),
                vm((2, 8, 128), f32), vm((8, 128), f32), vm((2, 8, 128), f32), vm((8, 128), f32),
                vm((2, 9, 2, 8, 128), f32), vm((2, 9, 8, 128), f32), vm((2, 9, 2, 8, 128), f32),
                vm((2, 9, 8, 128), f32),
                vm((12, 24, 128), f32), vm((16, 24, 128), f32), vm((16, 24, 128), f32), vm((3, 16, 24, 128), f32),
                vm((1, 12, 24, 128), f32), vm((1, 16, 24, 128), f32), vm((1, 16, 24, 128), f32),
                vm((3, 16, 24, 128), f32), vm((5, 12, 24, 128), f32),
                vm((3, 8, 8, 128), f32), vm((16, 128), f32), vm((16, 128), f32),
                vm((5, 2, 8, 24, 128), f32), vm((3, 2, 8, 24, 128), f32), vm((nx + ny + na, 8, 128), f32),
                pltpu.SemaphoreType.DMA((copies,)), pltpu.SemaphoreType.DMA((copies,)),
            ],
            compiler_params=pltpu.CompilerParams(
                collective_id=0, has_side_effects=True, vmem_limit_bytes=48 * 1024 * 1024),
        )(fixed, moving, disp, offs)
        return sim.reshape(()), out

    in_specs = (P("gx", "gy", "ga"), P("gx", "gy", "ga"), P(None, "gx", "gy", "ga"), P(None, "gx", "gy", "ga"))
    return jax.shard_map(on_device, mesh=mesh, in_specs=in_specs,
                         out_specs=(P(), P(None, "gx", "gy", "ga")), check_vma=False)
```

```python
import functools
import jax
import jax.numpy as jnp
from jax import lax
from jax.experimental import pallas as pl
from jax.experimental.pallas import tpu as pltpu
from jax.sharding import PartitionSpec as P

window_count = 729.0
epsilon = 1e-05
MESH = pl.DeviceIdType.MESH
HIGHEST = lax.Precision.HIGHEST
NINE = [(dx, dy) for dx in (0, -1, 1) for dy in (0, -1, 1)]
PLANE = [(dx, dy) for dx in (-1, 0, 1) for dy in (-1, 0, 1) if (dx, dy) != (0, 0)]


def iota(shape, dim):
    return lax.broadcasted_iota(jnp.int32, shape, dim)


def dot(a, b):
    return jnp.dot(a, b, precision=HIGHEST, preferred_element_type=jnp.float32)


def as_float(mask):
    return jnp.where(mask, 1.0, 0.0).astype(jnp.float32)


def shifted(v, halo, s, lane):
    n = v.shape[-1]
    if s == 0:
        return v
    if s > 0:
        return pltpu.roll(jnp.where(lane < s, halo, v), n - s, v.ndim - 1)
    return pltpu.roll(jnp.where(lane >= n + s, halo, v), -s, v.ndim - 1)


def tent(diff):
    return jnp.where(diff == 0, 0.5, jnp.where(jnp.abs(diff) == 1, 0.25, 0.0))


def plane_filter():
    r = iota((16, 144), 0)
    c = iota((16, 144), 1)
    slot = c >> 4
    q = c & 15
    sx = jnp.where(slot >= 6, 2, jnp.where(slot >= 3, 1, 0))
    sy = slot - 3 * sx
    wx = tent(2 * sx + ((q >> 1) & 1) - 2 - ((r >> 1) & 1))
    wy = tent(2 * sy + (q & 1) - 2 - (r & 1))
    return jnp.where((r >> 2) == (q >> 2), wx * wy, 0.0).astype(jnp.float32)


def box_rows(v):
    s2 = v[:-1] + v[1:]
    s4 = s2[:-2] + s2[2:]
    s8 = s4[:-4] + s4[4:]
    return s8[:8] + v[8:16]


def kernel(sizes, count, fixed_any, moving_any, disp_any, offs_any, sim_ref, out_ref,
           fixed_ref, moving_ref, disp_ref, offs_ref, local,
           cin, cslot, gslot, gsrc, edge_i, edge_j, edge_k, edge_g, zi_, zj_, zk_, zg_, hm, hf, hj, hk, mext, fext, jext, cext,
           shifts, slopes, smooth, offsets, tbox, tcoef, sims, send, recv):
    nx, ny, na = sizes
    me = {"gx": lax.axis_index("gx"), "gy": lax.axis_index("gy"), "ga": lax.axis_index("ga")}
    size = {"gx": nx, "gy": ny, "ga": na}
    pending = []
    counter = [0]
    known = {}

    def target(**moves):
        return {a: me[a] + moves.get(a, 0) for a in me}

    def exists(moves):
        key = tuple(moves.get(a, 0) for a in me)
        if key not in known:
            known[key] = inside(moves)
        return known[key]

    def inside(moves):
        conds = [((me[a] + d) >= 0) & ((me[a] + d) < size[a]) for a, d in moves.items() if d]
        return functools.reduce(jnp.logical_and, conds)

    def start(src, dst, moves):
        i = counter[0]
        counter[0] += 1
        c = pltpu.make_async_remote_copy(src, dst, send.at[i], recv.at[i],
                                         device_id=target(**moves), device_id_type=MESH)
        to = exists(moves)
        origin = exists({a: -d for a, d in moves.items()})
        pl.when(to)(c.start)
        pending.append((c, tuple(moves.get(a, 0) for a in me)))
        return c, origin

    def arrive(copies):
        for c, origin in copies:
            pl.when(origin)(c.wait_recv)

    def along(src, dst):
        return [start(src, dst.at[i, (1 - dx) * 3 + 1 - dy], {"gx": dx, "gy": dy, "ga": dz})
                for dx, dy in NINE for i, dz in ((0, 1), (1, -1))]

    def across(ext, lead, h):
        copies = []
        for dx, dy in PLANE:
            n = 8 if dx == 0 else h
            src0 = h + (8 - h if dx == 1 else 0)
            dst0 = {1: 0, 0: h, -1: h + 8}[dx]
            wide = 8 if dy == 0 else 4
            srcy = 12 if dy == 1 else 8
            dsty = {1: 4, 0: 8, -1: 16}[dy]
            src = ext.at[lead, pl.ds(src0, n), pl.ds(srcy, wide), :]
            dst = ext.at[lead, pl.ds(dst0, n), pl.ds(dsty, wide), :]
            copies.append(start(src, dst, {"gx": dx, "gy": dy}))
        return copies

    def slots(ref):
        return [start(ref.at[4], ref.at[(1 - dx) * 3 + 1 - dy], {"gx": dx, "gy": dy}) for dx, dy in PLANE]

    def line(axis, base, tile):
        sims[base] = tile
        copies = []
        n = size[axis]
        for d in range(1, n):
            i = counter[0]
            counter[0] += 1
            dev = dict(me)
            dev[axis] = lax.rem(me[axis] + d, n)
            c = pltpu.make_async_remote_copy(sims.at[base], sims.at[base + d], send.at[i], recv.at[i],
                                             device_id=dev, device_id_type=MESH)
            c.start()
            pending.append((c, None))
            copies.append(c)
        return copies

    def line_sum(axis, base, copies):
        total = sims[base]
        for d, c in enumerate(copies):
            c.wait_recv()
            total = total + sims[base + 1 + d]
        return total

    lane1 = iota((8, 128), 1)

    def pack(rows):
        tile = jnp.zeros((8, 128), jnp.float32)
        for i, v in enumerate(rows):
            tile = jnp.where((lane1 >> 3) == i, pltpu.roll(v, (4 + 8 * i) % 128, 1), tile)
        return tile

    def merged(i):
        z, part = i
        if part is None:
            return lambda q: jnp.where((lane1 & 7) < 4, z[0, q], z[1, q])
        return lambda q: jnp.where((lane1 & 7) < 4, z[0, q, part], z[1, q, part])

    def unpack(tile, i):
        return pltpu.roll(tile, (124 - 8 * i) % 128, 1)

    def halo_rows(ref, q, h, first):
        for sy in range(3):
            for sx, x0, n, d0 in ((0, 8 - h, h, 0), (1, 0, 8, h), (2, 0, h, h + 8)):
                tile = q(3 * sx + sy)
                for x in range(n):
                    ref[d0 + x, pl.ds(8 * sy, 8), :] = unpack(tile, first + x0 + x)

    def smooth_z(slots_ref, q):
        rows = []
        for slot in range(9):
            tile = q(slot)
            u = slots_ref[slot]
            uh = jnp.concatenate([unpack(tile, 0), unpack(tile, 1)], axis=0)
            rows.append(0.25 * (shifted(u, uh, -4, lane2) + 2.0 * u + shifted(u, uh, 4, lane2)))
        return jnp.concatenate(rows, axis=0)

    loads = [pltpu.make_async_copy(a, b, local.at[i]) for i, (a, b) in enumerate(
        ((disp_any, disp_ref), (offs_any, offs_ref), (moving_any, moving_ref), (fixed_any, fixed_ref)))]
    for c in loads:
        c.start()
    lane2 = iota((16, 128), 1)

    for ref in (zi_, zj_, zk_, zg_, mext, fext, jext, cext, cslot, gslot, gsrc, cin):
        ref[...] = jnp.zeros(ref.shape, ref.dtype)

    barrier = pltpu.get_barrier_semaphore()
    expected = nx - 1 + ny - 1 + na - 1
    for axis in ("gx", "gy", "ga"):
        for d in range(1, size[axis]):
            dev = dict(me)
            dev[axis] = lax.rem(me[axis] + d, size[axis])
            pl.semaphore_signal(barrier, inc=1, device_id=dev, device_id_type=MESH)
    for dx, dy in NINE:
        for dz in (-1, 0, 1):
            if (dx != 0) + (dy != 0) + (dz != 0) < 2:
                continue
            moves = {"gx": dx, "gy": dy, "ga": dz}
            cond = exists(moves)
            expected = expected + jnp.where(cond, 1, 0)

            def greet(moves=moves):
                pl.semaphore_signal(barrier, inc=1, device_id=target(**moves), device_id_type=MESH)

            pl.when(cond)(greet)

    for c in loads:
        c.wait()
    for k in range(3):
        for cx in range(2):
            cin[0, pl.ds(4 * k + 2 * cx, 2), :] = disp_ref[k, cx]
            cin[1, pl.ds(4 * k + 2 * cx, 2), :] = offs_ref[k, cx].astype(jnp.float32)
    spread = as_float(iota((32, 128), 0) == (iota((32, 128), 1) >> 2))
    cslot[4] = dot(cin[0], spread)
    offsets[...] = dot(cin[1], spread)
    mext[0, pl.ds(2, 8), pl.ds(8, 8), :] = moving_ref[...]
    edge_i[1] = pack([cslot[4, 0:8], cslot[4, 8:16]])
    edge_i[0] = pack([moving_ref[i] for i in range(8)] + [fixed_ref[i] for i in range(8)])
    fext[0, pl.ds(4, 8), pl.ds(8, 8), :] = fixed_ref[...]
    pl.semaphore_wait(barrier, expected)

    z_i = along(edge_i, zi_)
    c_slots = slots(cslot)
    m_center = across(mext, 0, 2)
    f_center = across(fext, 0, 4)
    filt = plane_filter()
    arrive(c_slots)
    arrive(z_i)
    smooth[...] = jax.nn.sigmoid(dot(filt, smooth_z(cslot, merged((zi_, 1)))))
    halo_rows(hm, merged((zi_, 0)), 2, 0)
    arrive(m_center)
    lane_m = iota((12, 24, 128), 2)
    mv = mext[0]
    mh = hm[...]
    for iz in range(5):
        shifts[iz] = shifted(mv, mh, iz - 2, lane_m)

    low = iota((8, 128), 0) < 4

    def warp_row(r, carry):
        cx = r // 4
        weights = []
        for k in range(3):
            row = 4 * k + 2 * cx
            frac = jnp.where(low, smooth[pl.ds(row, 1), :], smooth[pl.ds(row + 1, 1), :])
            off = jnp.where(low, offsets[pl.ds(row, 1), :], offsets[pl.ds(row + 1, 1), :])
            pairs = []
            for shift in range(-2, 3):
                lower = off == float(shift)
                upper = off == float(shift - 1)
                w = jnp.where(lower, 1.0 - frac, jnp.where(upper, frac, 0.0))
                d = jnp.where(lower, -1.0, jnp.where(upper, 1.0, 0.0))
                pairs.append((w, d))
            weights.append(pairs)
        acc = None
        for ix in range(5):
            mid = None
            for iy in range(5):
                inner = None
                for iz in range(5):
                    v = shifts[iz, r + ix, pl.ds(6 + iy, 8), :]
                    wz, dz = weights[2][iz]
                    t = (wz * v, dz * v)
                    inner = t if inner is None else (inner[0] + t[0], inner[1] + t[1])
                wy, dy = weights[1][iy]
                t = (wy * inner[0], dy * inner[0], wy * inner[1])
                mid = t if mid is None else tuple(a + b for a, b in zip(mid, t))
            wx, dx = weights[0][ix]
            t = (wx * mid[0], dx * mid[0], wx * mid[1], wx * mid[2])
            acc = t if acc is None else tuple(a + b for a, b in zip(acc, t))
        jext[0, r + 4, pl.ds(8, 8), :] = acc[0]
        slopes[0, r] = acc[1]
        slopes[1, r] = acc[2]
        slopes[2, r] = acc[3]
        return carry

    lax.fori_loop(0, 8, warp_row, 0)

    edge_j[...] = pack([jext[0, 4 + i, pl.ds(8, 8), :] for i in range(8)])
    z_j = along(edge_j, zj_)
    j_center = across(jext, 0, 4)
    halo_rows(hf, merged((zi_, 0)), 4, 8)
    arrive(f_center)
    for half in range(2):
        f = (fext[0], hf[...])[half]
        tbox[0, half] = box_rows(f)
        tbox[2, half] = box_rows(f * f)
    zi = iota((256, 128), 0)
    zo = iota((256, 128), 1)
    band = as_float(((zi < 128) & (jnp.abs(zi - zo) <= 4))
                    | ((zi >= 128) & ((jnp.abs(zi - zo) <= 4) | (jnp.abs(zi - 256 - zo) <= 4))))

    def box_y(ref):
        total = ref[:, pl.ds(4, 8), :]
        for s in range(5, 13):
            total = total + ref[:, pl.ds(s, 8), :]
        return total

    arrive(z_j)
    halo_rows(hj, merged((zj_, None)), 4, 0)
    arrive(j_center)
    for half in range(2):
        f = (fext[0], hf[...])[half]
        j = (jext[0], hj[...])[half]
        tbox[1, half] = box_rows(j)
        tbox[3, half] = box_rows(j * j)
        tbox[4, half] = box_rows(f * j)
    sums = []
    for q in range(5):
        both = [box_y(tbox.at[q, half]).reshape(64, 128) for half in range(2)]
        sums.append(dot(jnp.concatenate(both, axis=1), band).reshape(8, 8, 128))
    fs, js = sums[0], sums[1]
    cross = sums[4] - fs * js / window_count
    fvar = sums[2] - fs * fs / window_count
    wvar = sums[3] - js * js / window_count
    den = fvar * wvar + epsilon
    inv = 1.0 / den
    ratio = cross * inv
    similar = cross * ratio
    ca = 2.0 * ratio
    cb = -(ratio * ratio) * fvar
    cc = -(ca * fs + 2.0 * cb * js) / window_count
    rows = [ca[i] for i in range(8)] + [cb[i] for i in range(8)]
    edge_k[0] = pack(rows)
    edge_k[1] = pack([cc[i] for i in range(8)])
    z_k = along(edge_k, zk_)
    for q, v in enumerate((ca, cb, cc)):
        cext[q, pl.ds(4, 8), pl.ds(8, 8), :] = v
    c_copies = across(cext, pl.ds(0, 3), 4)
    s_a = line("ga", 0, jnp.sum(similar, axis=0))
    s_x = line("gx", na, line_sum("ga", 0, s_a))
    arrive(z_k)
    for q in range(3):
        halo_rows(hk.at[q], merged((zk_, q // 2)), 4, 8 * (q % 2))
        tcoef[q, 1] = box_rows(hk[q])
    arrive(c_copies)
    boxed = []
    for q in range(3):
        tcoef[q, 0] = box_rows(cext[q])
    for q in range(3):
        both = [box_y(tcoef.at[q, half]).reshape(64, 128) for half in range(2)]
        boxed.append(dot(jnp.concatenate(both, axis=1), band).reshape(8, 8, 128))
    grad = -(fixed_ref[...] * boxed[0] + 2.0 * jext[0, pl.ds(4, 8), pl.ds(8, 8), :] * boxed[1] + boxed[2])
    for k in range(3):
        t = grad * slopes[k]
        for cx in range(2):
            part = jnp.sum(t[4 * cx:4 * cx + 4], axis=0)
            for cy in range(2):
                row = jnp.sum(jnp.where(low == (cy == 0), part, 0.0), axis=0, keepdims=True)
                gsrc[pl.ds(4 * k + 2 * cx + cy, 1), :] = row
    group = as_float((iota((128, 128), 0) >> 2) == (iota((128, 128), 1) >> 2))
    s = smooth[...]
    u = dot(gsrc[...], group) * s * (1.0 - s)
    gslot[4] = u
    edge_g[...] = pack([u[:8], u[8:]])
    z_g = along(edge_g, zg_)
    g_slots = slots(gslot)
    s_y = line("gy", na + nx, line_sum("gx", na, s_x))
    total = line_sum("gy", na + nx, s_y)
    sim_ref[...] = (jnp.sum(total) / count).reshape(1, 1)
    arrive(g_slots)
    arrive(z_g)
    pick = as_float(iota((128, 32), 0) == (iota((128, 32), 1) << 2))
    final = dot(dot(filt, smooth_z(gslot, merged((zg_, None)))), pick)
    for k in range(3):
        for cx in range(2):
            out_ref[k, cx] = final[4 * k + 2 * cx:4 * k + 2 * cx + 2]
    groups = {}
    for c, key in pending:
        groups.setdefault(key, []).append(c)
    for key, group in groups.items():

        def finish(group=group):
            for c in group:
                c.wait_send()

        if key is None:
            finish()
        else:
            pl.when(known[key])(finish)


def solution(mesh):
    nx, ny, na = mesh.shape["gx"], mesh.shape["gy"], mesh.shape["ga"]

    def on_device(fixed, moving, disp, offs):
        count = float(fixed.size * nx * ny * na)
        f32 = jnp.float32
        vm = pltpu.VMEM
        copies = 192 + nx + ny + na
        sim, out = pl.pallas_call(
            functools.partial(kernel, (nx, ny, na), count),
            out_shape=(jax.ShapeDtypeStruct((1, 1), f32), jax.ShapeDtypeStruct(disp.shape, f32)),
            in_specs=[pl.BlockSpec(memory_space=pltpu.HBM)] * 4,
            out_specs=(pl.BlockSpec(memory_space=pltpu.VMEM),) * 2,
            scratch_shapes=[
                vm(fixed.shape, f32), vm(moving.shape, f32), vm(disp.shape, f32), vm(offs.shape, jnp.int32),
                pltpu.SemaphoreType.DMA((4,)),
                vm((2, 16, 32), f32), vm((9, 16, 128), f32), vm((9, 16, 128), f32), vm((16, 128), f32),
                vm((2, 8, 128), f32), vm((8, 128), f32), vm((2, 8, 128), f32), vm((8, 128), f32),
                vm((2, 9, 2, 8, 128), f32), vm((2, 9, 8, 128), f32), vm((2, 9, 2, 8, 128), f32),
                vm((2, 9, 8, 128), f32),
                vm((12, 24, 128), f32), vm((16, 24, 128), f32), vm((16, 24, 128), f32), vm((3, 16, 24, 128), f32),
                vm((1, 12, 24, 128), f32), vm((1, 16, 24, 128), f32), vm((1, 16, 24, 128), f32),
                vm((3, 16, 24, 128), f32), vm((5, 12, 24, 128), f32),
                vm((3, 8, 8, 128), f32), vm((16, 128), f32), vm((16, 128), f32),
                vm((5, 2, 8, 24, 128), f32), vm((3, 2, 8, 24, 128), f32), vm((nx + ny + na, 8, 128), f32),
                pltpu.SemaphoreType.DMA((copies,)), pltpu.SemaphoreType.DMA((copies,)),
            ],
            compiler_params=pltpu.CompilerParams(
                collective_id=0, has_side_effects=True, vmem_limit_bytes=48 * 1024 * 1024),
        )(fixed, moving, disp, offs)
        return sim.reshape(()), out

    in_specs = (P("gx", "gy", "ga"), P("gx", "gy", "ga"), P(None, "gx", "gy", "ga"), P(None, "gx", "gy", "ga"))
    return jax.shard_map(on_device, mesh=mesh, in_specs=in_specs,
                         out_specs=(P(), P(None, "gx", "gy", "ga")), check_vma=False)
```
